32 devices in a mesh: outer: 4 (over y, x), node: 8 (over z, core).
Axes of the slice: x: 2, y: 2, z: 4, core: 2. Of those that a mesh axis runs over, the one named last changes fastest.
Arguments:
- activations: bfloat16 [8192, 768], P(('outer', 'node')), may hold values from -6 to 6
- upstream: bfloat16 [8192, 4096], P(('outer', 'node')), may hold values from -0.13183594 to 0.13183594
- combine: float32 [8192], P(('outer', 'node')), may hold values from 0.05 to 1
- counts: int32 [32], P(('outer', 'node')), may hold values from 64 to 256, as said below
Outputs:
- weight_grad: float32 [768, 4096], P(('node', 'outer'))
The draws below stay inside these ranges and needn't reach their ends.
Inputs may be any that keep to these rules, and one draw needn't show every extreme that they name: counts[i] is the number of filled slots of device i; slots at or after it are padding. Some device is full in every draw.
All inputs are finite; a program needn't handle non-finite values.
Results may differ from the reference program's by a relative error of at most 0.014.
Values may be sent and summed in bfloat16 or wider, within the bound.
A program may use at most 64 MiB of HBM per device.

```python
import math
import jax
import jax.numpy as jnp
from jax import lax

D = 4096
FFW = 768
BLOCK = 128
TOK_DEV = 256
ROWS = 8192
N_OUTER = 4
N_NODE = 8
DEVICES = 32


def draw_counts(key, part):
    key = jax.random.fold_in(key, 7)
    first, second = jax.random.split(key)
    values = jax.random.randint(first, (DEVICES,), TOK_DEV // 4, TOK_DEV + 1).astype(jnp.int32)
    where_full = jax.random.randint(second, (), 0, DEVICES)
    return values.at[where_full].set(TOK_DEV).astype(jnp.int32)


def block_scale(own_key, shape, shards, low, high):
    factor_of = 1.0
    for dim, parts in shards:
        steps = jax.random.uniform(jax.random.fold_in(jax.random.fold_in(own_key, 6), dim), (parts,), jnp.float32, low / len(shards), high / len(shards))
        factor_of = factor_of * jnp.repeat(jnp.exp(steps), shape[dim] // parts).reshape((-1,) + (1,) * (len(shape) - 1 - dim))
    return factor_of


def gaussian(own_key, extent, deviation, reach, shards=(), kind=jnp.bfloat16):
    entries = deviation * jax.random.normal(own_key, extent, jnp.float32)
    if shards:
        entries = entries * block_scale(own_key, extent, shards, -0.22, 0.18)
    return jnp.clip(entries, -reach, reach).astype(kind)


def setup_inputs(seed: int = 0) -> dict:
    key_of = jax.random.split(jax.random.key(seed), 5)
    return {
        "activations": gaussian(key_of[0], (ROWS, FFW), 1.0, 6.0, ((0, 32),)),
        "upstream": gaussian(key_of[1], (ROWS, D), (2.0 / (TOK_DEV * DEVICES) ** 0.5), 0.13183594, ((0, 32),)),
        "combine": jnp.clip(jnp.exp(math.log(1.0) - 2.9957323 * jax.random.uniform(key_of[2], (ROWS,), jnp.float32) ** block_scale(key_of[2], (ROWS,), ((0, 32),), -0.2, 0.2)), 0.05, 1.0),
        "counts": draw_counts(jax.random.fold_in(key_of[4], 71), 0),
    }


def reference(activations, upstream, combine, counts):
    acts = activations.reshape(N_OUTER, N_NODE, TOK_DEV, FFW)
    ups = upstream.reshape(N_OUTER, N_NODE, TOK_DEV, D)
    weights = combine.reshape(N_OUTER, N_NODE, TOK_DEV)
    filled = counts.reshape(N_OUTER, N_NODE)
    slot = jnp.arange(TOK_DEV, dtype=jnp.int32)
    live = slot[None, None, :] < filled[:, :, None]
    factor = jnp.where(live, weights, jnp.zeros_like(weights))
    scaled = (ups.astype(jnp.float32) * factor[..., None]).astype(jnp.bfloat16)

    def node_step(total, pair):
        left, right = pair
        partial_value = lax.dot_general(left, right, (((0,), (0,)), ((), ())), preferred_element_type=jnp.float32)
        partial_value = lax.optimization_barrier(partial_value.astype(jnp.bfloat16))
        return total + partial_value.astype(jnp.float32), None

    def outer_step(total, pair):
        left, right = pair
        replica, _ = lax.scan(node_step, jnp.zeros((FFW, D), jnp.float32), (left, right))
        blocks = replica.reshape(FFW, D // BLOCK, BLOCK)
        amax = jnp.max(jnp.abs(blocks), axis=2) + 1e-6
        scale = lax.optimization_barrier(amax.astype(jnp.bfloat16)).astype(jnp.float32)
        quant = lax.optimization_barrier((blocks / scale[..., None]).astype(jnp.bfloat16))
        back = quant.astype(jnp.float32) * scale[..., None]
        return total + back.reshape(FFW, D), None

    result, _ = lax.scan(outer_step, jnp.zeros((FFW, D), jnp.float32), (acts, scaled))
    return result
```

```python
import functools
import jax
import jax.numpy as jnp
from jax import lax
from jax.experimental import pallas as pl
from jax.experimental.pallas import tpu as pltpu
from jax.sharding import PartitionSpec as P

BLOCK = 128
CHUNK = 256
HOP_LAG = 1
SUM_LAG = 1
MESH = pl.DeviceIdType.MESH


def plain_body(activations, upstream, combine, counts):
    slots = activations.shape[0]
    width = upstream.shape[1]
    live = lax.iota(jnp.int32, slots) < counts[0]
    factor = jnp.where(live, combine, jnp.zeros_like(combine))
    scaled = (upstream.astype(jnp.float32) * factor[:, None]).astype(jnp.bfloat16)
    shard_rows = activations.shape[1] // lax.axis_size("node")
    partial_value = lax.dot_general(
        activations, scaled, (((0,), (0,)), ((), ())), preferred_element_type=jnp.float32
    )
    replica = lax.psum_scatter(
        partial_value.astype(jnp.bfloat16), "node", scatter_dimension=0, tiled=True
    ).astype(jnp.float32)
    blocks = replica.reshape(shard_rows, width // BLOCK, BLOCK)
    amax = jnp.max(jnp.abs(blocks), axis=2) + 1e-06
    scale_low = lax.optimization_barrier(amax.astype(jnp.bfloat16))
    quant = (blocks / scale_low.astype(jnp.float32)[..., None]).astype(jnp.bfloat16)
    quant = quant.reshape(shard_rows, width)
    got_quant, got_scale = (
        lax.all_to_all(quant, "outer", split_axis=0, concat_axis=0, tiled=True),
        lax.all_to_all(scale_low, "outer", split_axis=0, concat_axis=0, tiled=True),
    )
    sources = lax.axis_size("outer")
    owned = shard_rows // sources
    values = got_quant.astype(jnp.float32).reshape(sources, owned, width // BLOCK, BLOCK)
    scales = got_scale.astype(jnp.float32).reshape(sources, owned, width // BLOCK)
    restored = values * scales[..., None]
    return jnp.sum(restored, axis=0).reshape(owned, width)


def kernel(
    n_outer, n_node, chunks, w,
    acts_ref, up_ref, combine_ref, counts_ref, out_ref,
    acts_t, mine, theirs, part, got, summed, back, to_peers, from_peers, to_owners,
    a_send, a_recv, s_send, s_recv, z_send, z_recv, c_send, c_recv, d_send, d_recv,
):
    slots = acts_ref.shape[0]
    line = n_node // 2
    half = acts_t.shape[1] // 2
    groups = n_node // 2
    owned = out_ref.shape[0]
    group_rows = owned * n_outer
    cols = chunks * w
    o = lax.axis_index("outer")
    n = lax.axis_index("node")
    c, k = n // 2, n % 2
    sibling = c * 2 + (1 - k)
    at_end = jnp.logical_or(c == 0, c == line - 1)
    side = jnp.where(c == 0, 0, 1)

    barrier = pltpu.get_barrier_semaphore()
    for step in range(1, n_node):
        pl.semaphore_signal(
            barrier, inc=1, device_id=(o, lax.rem(n + step, n_node)), device_id_type=MESH
        )
    for step in range(1, n_outer):
        pl.semaphore_signal(
            barrier, inc=1, device_id=(lax.rem(o + step, n_outer), n), device_id_type=MESH
        )

    acts_t[0] = acts_ref[...].T
    live = lax.broadcasted_iota(jnp.int32, (1, slots), 1) < counts_ref[0]
    factor = jnp.where(live, combine_ref[...], 0.0)
    factor = jnp.broadcast_to(factor, (BLOCK, slots)).T

    def scaled(column):
        parts = []
        for b in range(w // BLOCK):
            at = pl.ds(pl.multiple_of(column + b * BLOCK, BLOCK), BLOCK)
            parts.append((up_ref[:, at].astype(jnp.float32) * factor).astype(jnp.bfloat16))
        return jnp.concatenate(parts, axis=1) if len(parts) > 1 else parts[0]

    @pl.loop(0, chunks)
    def _(j):
        theirs[j] = scaled((1 - k) * cols + j * w)

    pl.semaphore_wait(barrier, n_node + n_outer - 2)

    def acts_copy():
        return pltpu.make_async_remote_copy(
            src_ref=acts_t.at[0], dst_ref=acts_t.at[1], send_sem=a_send, recv_sem=a_recv,
            device_id=(o, sibling), device_id_type=MESH,
        )

    def scaled_copy(j):
        return pltpu.make_async_remote_copy(
            src_ref=theirs.at[j], dst_ref=mine.at[1, j],
            send_sem=s_send.at[j], recv_sem=s_recv.at[j],
            device_id=(o, sibling), device_id_type=MESH,
        )

    def chain_copy(way, j, source):
        onward = c - 1 if way == 0 else c + 1
        return pltpu.make_async_remote_copy(
            src_ref=source.at[way, j], dst_ref=got.at[way, j],
            send_sem=z_send.at[way, j], recv_sem=z_recv.at[way, j],
            device_id=(o, onward * 2 + k), device_id_type=MESH,
        )

    def peer_copy(j, to, slot):
        return pltpu.make_async_remote_copy(
            src_ref=to_peers.at[j, to], dst_ref=from_peers.at[j, slot],
            send_sem=c_send.at[j, to], recv_sem=c_recv.at[j, slot],
            device_id=(to, n), device_id_type=MESH,
        )

    def owner_copy(j, g, core, owner):
        at = pl.ds(pl.multiple_of(core * cols + j * w, BLOCK), w)
        return pltpu.make_async_remote_copy(
            src_ref=to_owners.at[j, g], dst_ref=out_ref.at[:, at],
            send_sem=d_send.at[j, g], recv_sem=d_recv.at[core, j],
            device_id=(o, owner), device_id_type=MESH,
        )

    acts_copy().start()

    @pl.loop(0, chunks)
    def _(j):
        scaled_copy(j).start()

    @pl.loop(0, chunks)
    def _(j):
        mine[0, j] = scaled(k * cols + j * w)

    acts_copy().wait_recv()

    def chain_step(way, t):
        lag = (line - 1 - c if way == 0 else c) * HOP_LAG
        first = lag == 0
        last = lag == (line - 1) * HOP_LAG
        j = t - lag
        inside = jnp.logical_and(j >= 0, j < chunks)

        @pl.when(jnp.logical_and(inside, first))
        def _():
            chain_copy(way, j, part).start()

        @pl.when(jnp.logical_and(inside, jnp.logical_not(jnp.logical_or(first, last))))
        def _():
            chain_copy(way, j, part).wait_recv()
            summed[way, j] = (
                got[way, j].astype(jnp.float32) + part[way, j].astype(jnp.float32)
            ).astype(jnp.bfloat16)
            chain_copy(way, j, summed).start()

    def quantise_step(t):
        j = t - (line - 1) * HOP_LAG

        @pl.when(jnp.logical_and(at_end, jnp.logical_and(j >= 0, j < chunks)))
        def _():
            for way in range(2):

                @pl.when(side == way)
                def _(way=way):
                    chain_copy(way, j, part).wait_recv()

            for g in range(groups):
                rows = pl.ds(g * group_rows, group_rows)
                replica = got[side, j, rows, :].astype(jnp.float32) + part[
                    side, j, rows, :
                ].astype(jnp.float32)
                for b in range(w // BLOCK):
                    block = replica[:, b * BLOCK : (b + 1) * BLOCK]
                    amax = jnp.max(jnp.abs(block), axis=1, keepdims=True) + 1e-06
                    scale = amax.astype(jnp.bfloat16).astype(jnp.float32)
                    quant = (block / scale).astype(jnp.bfloat16)
                    back[rows, b * BLOCK : (b + 1) * BLOCK] = quant.astype(jnp.float32) * scale
            for to in range(n_outer):
                rows = [
                    back[g * group_rows + to * owned : g * group_rows + (to + 1) * owned, :]
                    for g in range(groups)
                ]
                rows = jnp.concatenate(rows, axis=0).astype(jnp.bfloat16)

                @pl.when(o == to)
                def _(rows=rows, to=to):
                    from_peers[j, to] = rows

                @pl.when(o != to)
                def _(rows=rows, to=to):
                    to_peers[j, to] = rows
                    peer_copy(j, to, o).start()

    def sum_step(t):
        j = t - (line - 1) * HOP_LAG - SUM_LAG

        @pl.when(jnp.logical_and(at_end, jnp.logical_and(j >= 0, j < chunks)))
        def _():
            for slot in range(n_outer):

                @pl.when(o != slot)
                def _(slot=slot):
                    peer_copy(j, lax.rem(o + 1, n_outer), slot).wait_recv()

            total = from_peers[j, 0].astype(jnp.float32)
            for slot in range(1, n_outer):
                total = total + from_peers[j, slot].astype(jnp.float32)
            for g in range(groups):
                owner = side * groups + g
                rows = total[g * owned : (g + 1) * owned, :]

                @pl.when(owner == n)
                def _(rows=rows):
                    at = pl.ds(pl.multiple_of(k * cols + j * w, BLOCK), w)
                    out_ref[:, at] = rows

                @pl.when(owner != n)
                def _(rows=rows, g=g, owner=owner):
                    to_owners[j, g] = rows
                    owner_copy(j, g, k, owner).start()

    @pl.loop(0, chunks + (line - 1) * HOP_LAG + SUM_LAG)
    def _(t):
        @pl.when(t < chunks)
        def _():
            scaled_copy(t).wait_recv()
            value = jnp.dot(
                acts_t[0], mine[0, t], preferred_element_type=jnp.float32
            ) + jnp.dot(acts_t[1], mine[1, t], preferred_element_type=jnp.float32)
            value = value.astype(jnp.bfloat16)
            part[0, t] = value[:half]
            part[1, t] = value[half:]

        chain_step(0, t)
        chain_step(1, t)
        quantise_step(t)
        sum_step(t)

    end_chip = jnp.where(n < groups, 0, line - 1)

    acts_copy().wait_send()

    @pl.loop(0, chunks)
    def _(j):
        scaled_copy(j).wait_send()

        @pl.when(c > 0)
        def _():
            chain_copy(0, j, part).wait_send()

        @pl.when(c < line - 1)
        def _():
            chain_copy(1, j, part).wait_send()

        @pl.when(at_end)
        def _():
            for to in range(n_outer):

                @pl.when(o != to)
                def _(to=to):
                    peer_copy(j, to, o).wait_send()

            for g in range(groups):

                @pl.when(side * groups + g != n)
                def _(g=g):
                    owner_copy(j, g, k, sibling).wait_send()

        for core in range(2):

            @pl.when(end_chip * 2 + core != n)
            def _(core=core):
                owner_copy(j, 0, core, sibling).wait_recv()


def fused_body(n_outer, n_node, activations, upstream, combine, counts):
    slots, ffw = activations.shape
    width = upstream.shape[1]
    owned = ffw // (n_outer * n_node)
    half, cols = ffw // 2, width // 2
    w = CHUNK
    chunks = cols // w
    groups = n_node // 2
    dma = pltpu.SemaphoreType.DMA
    vmem = pltpu.VMEM
    return pl.pallas_call(
        functools.partial(kernel, n_outer, n_node, chunks, w),
        out_shape=jax.ShapeDtypeStruct((owned, width), jnp.float32),
        in_specs=[pl.BlockSpec(memory_space=pltpu.VMEM)] * 3
        + [pl.BlockSpec(memory_space=pltpu.SMEM)],
        out_specs=pl.BlockSpec(memory_space=pltpu.VMEM),
        scratch_shapes=[
            vmem((2, ffw, slots), jnp.bfloat16),
            vmem((2, chunks, slots, w), jnp.bfloat16),
            vmem((chunks, slots, w), jnp.bfloat16),
            vmem((2, chunks, half, w), jnp.bfloat16),
            vmem((2, chunks, half, w), jnp.bfloat16),
            vmem((2, chunks, half, w), jnp.bfloat16),
            vmem((half, w), jnp.float32),
            vmem((chunks, n_outer, groups * owned, w), jnp.bfloat16),
            vmem((chunks, n_outer, groups * owned, w), jnp.bfloat16),
            vmem((chunks, groups, owned, w), jnp.float32),
            dma, dma,
            dma((chunks,)), dma((chunks,)),
            dma((2, chunks)), dma((2, chunks)),
            dma((chunks, n_outer)), dma((chunks, n_outer)),
            dma((chunks, groups)), dma((2, chunks)),
        ],
        compiler_params=pltpu.CompilerParams(
            collective_id=0, has_side_effects=True, vmem_limit_bytes=56 * 1024 * 1024
        ),
        cost_estimate=pl.CostEstimate(
            flops=2 * slots * ffw * width, bytes_accessed=8 << 20, transcendentals=0
        ),
    )(activations, upstream, combine.reshape(1, slots), counts)


def solution(mesh):
    n_outer, n_node = mesh.shape["outer"], mesh.shape["node"]

    def body(activations, upstream, combine, counts):
        ffw, width = activations.shape[1], upstream.shape[1]
        owned = ffw // (n_outer * n_node)
        fits = (
            n_node >= 4
            and owned % 8 == 0
            and (owned * n_outer) % 16 == 0
            and (owned * n_node // 2) % 16 == 0
            and (width // 2) % CHUNK == 0
        )
        if fits:
            return fused_body(n_outer, n_node, activations, upstream, combine, counts)
        return plain_body(activations, upstream, combine, counts)

    return jax.shard_map(
        body,
        mesh=mesh,
        in_specs=(
            P(("outer", "node"), None),
            P(("outer", "node"), None),
            P(("outer", "node")),
            P(("outer", "node")),
        ),
        out_specs=P(("node", "outer"), None),
        check_vma=False,
    )
```

```python
import functools
import jax
import jax.numpy as jnp
from jax import lax
from jax.experimental import pallas as pl
from jax.experimental.pallas import tpu as pltpu
from jax.sharding import PartitionSpec as P

BLOCK = 128
CHUNK = 128
PARTS = 1
HOP_LAG = 2
SUM_LAG = 3
MESH = pl.DeviceIdType.MESH


def plain_body(activations, upstream, combine, counts):
    slots = activations.shape[0]
    width = upstream.shape[1]
    live = lax.iota(jnp.int32, slots) < counts[0]
    factor = jnp.where(live, combine, jnp.zeros_like(combine))
    scaled = (upstream.astype(jnp.float32) * factor[:, None]).astype(jnp.bfloat16)
    shard_rows = activations.shape[1] // lax.axis_size("node")
    partial_value = lax.dot_general(
        activations, scaled, (((0,), (0,)), ((), ())), preferred_element_type=jnp.float32
    )
    replica = lax.psum_scatter(
        partial_value.astype(jnp.bfloat16), "node", scatter_dimension=0, tiled=True
    ).astype(jnp.float32)
    blocks = replica.reshape(shard_rows, width // BLOCK, BLOCK)
    amax = jnp.max(jnp.abs(blocks), axis=2) + 1e-06
    scale_low = lax.optimization_barrier(amax.astype(jnp.bfloat16))
    quant = (blocks / scale_low.astype(jnp.float32)[..., None]).astype(jnp.bfloat16)
    quant = quant.reshape(shard_rows, width)
    got_quant, got_scale = (
        lax.all_to_all(quant, "outer", split_axis=0, concat_axis=0, tiled=True),
        lax.all_to_all(scale_low, "outer", split_axis=0, concat_axis=0, tiled=True),
    )
    sources = lax.axis_size("outer")
    owned = shard_rows // sources
    values = got_quant.astype(jnp.float32).reshape(sources, owned, width // BLOCK, BLOCK)
    scales = got_scale.astype(jnp.float32).reshape(sources, owned, width // BLOCK)
    restored = values * scales[..., None]
    return jnp.sum(restored, axis=0).reshape(owned, width)


def kernel(
    n_outer, n_node, chunks, w,
    acts_ref, up_ref, combine_ref, counts_ref, out_ref,
    acts_t, mine, theirs, part, got, summed, back, to_peers, from_peers, stash, to_owners, from_ends,
    a_send, a_recv, s_send, s_recv, z_send, z_recv, c_send, c_recv, d_send, d_recv,
):
    slots = acts_ref.shape[0]
    line = n_node // 2
    half = acts_t.shape[1] // 2
    groups = n_node // 2
    units = PARTS * chunks
    part_groups = groups // PARTS
    owned = out_ref.shape[0]
    group_rows = owned * n_outer
    cols = chunks * w
    o = lax.axis_index("outer")
    n = lax.axis_index("node")
    c, k = n // 2, n % 2
    sibling = c * 2 + (1 - k)
    at_end = jnp.logical_or(c == 0, c == line - 1)
    side = jnp.where(c == 0, 0, 1)

    barrier = pltpu.get_barrier_semaphore()
    for step in range(1, n_node):
        pl.semaphore_signal(
            barrier, inc=1, device_id=(o, lax.rem(n + step, n_node)), device_id_type=MESH
        )
    for step in range(1, n_outer):
        pl.semaphore_signal(
            barrier, inc=1, device_id=(lax.rem(o + step, n_outer), n), device_id_type=MESH
        )

    acts_t[0] = acts_ref[...].T
    live = lax.broadcasted_iota(jnp.int32, (1, slots), 1) < counts_ref[0]
    factor = jnp.where(live, combine_ref[...], 0.0)
    factor = jnp.broadcast_to(factor, (BLOCK, slots)).T

    def scaled(column):
        parts = []
        for b in range(w // BLOCK):
            at = pl.ds(pl.multiple_of(column + b * BLOCK, BLOCK), BLOCK)
            parts.append((up_ref[:, at].astype(jnp.float32) * factor).astype(jnp.bfloat16))
        return jnp.concatenate(parts, axis=1) if len(parts) > 1 else parts[0]

    @pl.loop(0, chunks)
    def _(j):
        theirs[j] = scaled((1 - k) * cols + j * w)

    pl.semaphore_wait(barrier, n_node + n_outer - 2)

    def acts_copy():
        return pltpu.make_async_remote_copy(
            src_ref=acts_t.at[0], dst_ref=acts_t.at[1], send_sem=a_send, recv_sem=a_recv,
            device_id=(o, sibling), device_id_type=MESH,
        )

    def scaled_copy(j):
        return pltpu.make_async_remote_copy(
            src_ref=theirs.at[j], dst_ref=mine.at[1, j],
            send_sem=s_send.at[j], recv_sem=s_recv.at[j],
            device_id=(o, sibling), device_id_type=MESH,
        )

    def chain_copy(way, j, source):
        onward = c - 1 if way == 0 else c + 1
        return pltpu.make_async_remote_copy(
            src_ref=source.at[way, j], dst_ref=got.at[way, j],
            send_sem=z_send.at[way, j], recv_sem=z_recv.at[way, j],
            device_id=(o, onward * 2 + k), device_id_type=MESH,
        )

    def peer_copy(j, to, slot):
        return pltpu.make_async_remote_copy(
            src_ref=to_peers.at[j, to], dst_ref=from_peers.at[j, slot],
            send_sem=c_send.at[j, to], recv_sem=c_recv.at[j, slot],
            device_id=(to, n), device_id_type=MESH,
        )

    def owner_of(unit, g):
        p = unit // chunks
        return side * groups + jnp.where(side == 0, PARTS - 1 - p, p) * part_groups + g

    def owner_copy(pair, g, core, owner):
        q = lax.rem(pair, chunks // 2)
        return pltpu.make_async_remote_copy(
            src_ref=to_owners.at[pair, g], dst_ref=from_ends.at[core, q],
            send_sem=d_send.at[pair, g], recv_sem=d_recv.at[core, q],
            device_id=(o, owner), device_id_type=MESH,
        )

    acts_copy().start()

    @pl.loop(0, chunks)
    def _(j):
        scaled_copy(j).start()

    acts_copy().wait_recv()

    def chain_step(way, t):
        lag = (line - 1 - c if way == 0 else c) * HOP_LAG
        first = lag == 0
        last = lag == (line - 1) * HOP_LAG
        j = t - lag
        inside = jnp.logical_and(j >= 0, j < units)

        @pl.when(jnp.logical_and(inside, first))
        def _():
            chain_copy(way, j, part).start()

        @pl.when(jnp.logical_and(inside, jnp.logical_not(jnp.logical_or(first, last))))
        def _():
            chain_copy(way, j, part).wait_recv()
            summed[way, j] = (
                got[way, j].astype(jnp.float32) + part[way, j].astype(jnp.float32)
            ).astype(jnp.bfloat16)
            chain_copy(way, j, summed).start()

    def quantise_step(t):
        j = t - (line - 1) * HOP_LAG

        @pl.when(jnp.logical_and(at_end, jnp.logical_and(j >= 0, j < units)))
        def _():
            for way in range(2):

                @pl.when(side == way)
                def _(way=way):
                    chain_copy(way, j, part).wait_recv()

            for g in range(part_groups):
                rows = pl.ds(g * group_rows, group_rows)
                replica = got[side, j, rows, :].astype(jnp.float32) + part[
                    side, j, rows, :
                ].astype(jnp.float32)
                for b in range(w // BLOCK):
                    block = replica[:, b * BLOCK : (b + 1) * BLOCK]
                    amax = jnp.max(jnp.abs(block), axis=1, keepdims=True) + 1e-06
                    scale = amax.astype(jnp.bfloat16).astype(jnp.float32)
                    quant = (block / scale).astype(jnp.bfloat16)
                    back[rows, b * BLOCK : (b + 1) * BLOCK] = quant.astype(jnp.float32) * scale
            for to in range(n_outer):
                rows = [
                    back[g * group_rows + to * owned : g * group_rows + (to + 1) * owned, :]
                    for g in range(part_groups)
                ]
                rows = jnp.concatenate(rows, axis=0).astype(jnp.bfloat16)

                @pl.when(o == to)
                def _(rows=rows, to=to):
                    from_peers[j, to] = rows

                @pl.when(o != to)
                def _(rows=rows, to=to):
                    to_peers[j, to] = rows
                    peer_copy(j, to, o).start()

    def sum_step(t):
        j = t - (line - 1) * HOP_LAG - SUM_LAG

        @pl.when(jnp.logical_and(at_end, jnp.logical_and(j >= 0, j < units)))
        def _():
            for slot in range(n_outer):

                @pl.when(o != slot)
                def _(slot=slot):
                    peer_copy(j, lax.rem(o + 1, n_outer), slot).wait_recv()

            total = from_peers[j, 0].astype(jnp.float32)
            for slot in range(1, n_outer):
                total = total + from_peers[j, slot].astype(jnp.float32)
            for g in range(part_groups):
                owner = owner_of(j, g)
                rows = total[g * owned : (g + 1) * owned, :]

                @pl.when(owner == n)
                def _(rows=rows):
                    at = pl.ds(pl.multiple_of(k * cols + lax.rem(j, chunks) * w, BLOCK), w)
                    out_ref[:, at] = rows

                @pl.when(owner != n)
                def _(rows=rows, g=g):
                    stash[g, pl.ds(pl.multiple_of(lax.rem(j, 2) * owned, 8), owned), :] = rows

                @pl.when(jnp.logical_and(owner != n, lax.rem(j, 2) == 1))
                def _(g=g, owner=owner):
                    to_owners[j // 2, g] = stash[g].astype(jnp.bfloat16)
                    owner_copy(j // 2, g, k, owner).start()

    @pl.loop(0, units + (line - 1) * HOP_LAG + SUM_LAG)
    def _(t):
        @pl.when(t < chunks)
        def _():
            mine[0, t] = scaled(k * cols + t * w)
            scaled_copy(t).wait_recv()
            value = jnp.dot(
                acts_t[0], mine[0, t], preferred_element_type=jnp.float32
            ) + jnp.dot(acts_t[1], mine[1, t], preferred_element_type=jnp.float32)
            value = value.astype(jnp.bfloat16)
            size = half // PARTS
            for p in range(PARTS):
                low = (PARTS - 1 - p) * size
                part[0, p * chunks + t] = value[low : low + size]
                part[1, p * chunks + t] = value[half + p * size : half + (p + 1) * size]

        chain_step(0, t)
        chain_step(1, t)
        quantise_step(t)
        sum_step(t)

    end_chip = jnp.where(n < groups, 0, line - 1)

    acts_copy().wait_send()

    @pl.loop(0, units)
    def _(j):
        @pl.when(c > 0)
        def _():
            chain_copy(0, j, part).wait_send()

        @pl.when(c < line - 1)
        def _():
            chain_copy(1, j, part).wait_send()

        @pl.when(at_end)
        def _():
            for to in range(n_outer):

                @pl.when(o != to)
                def _(to=to):
                    peer_copy(j, to, o).wait_send()

            for g in range(part_groups):

                @pl.when(jnp.logical_and(owner_of(j, g) != n, lax.rem(j, 2) == 1))
                def _(g=g):
                    owner_copy(j // 2, g, k, sibling).wait_send()

    @pl.loop(0, chunks)
    def _(j):
        scaled_copy(j).wait_send()

    @pl.loop(0, chunks // 2)
    def _(q):
        for core in range(2):

            @pl.when(end_chip * 2 + core != n)
            def _(core=core):
                owner_copy(q, 0, core, sibling).wait_recv()
                both = from_ends[core, q].astype(jnp.float32)
                for b in range(2):
                    at = pl.ds(pl.multiple_of(core * cols + (2 * q + b) * w, BLOCK), w)
                    out_ref[:, at] = both[b * owned : (b + 1) * owned]


def fused_body(n_outer, n_node, activations, upstream, combine, counts):
    slots, ffw = activations.shape
    width = upstream.shape[1]
    owned = ffw // (n_outer * n_node)
    half, cols = ffw // 2, width // 2
    w = CHUNK
    chunks = cols // w
    units = PARTS * chunks
    part_groups = n_node // 2 // PARTS
    dma = pltpu.SemaphoreType.DMA
    vmem = pltpu.VMEM
    return pl.pallas_call(
        functools.partial(kernel, n_outer, n_node, chunks, w),
        out_shape=jax.ShapeDtypeStruct((owned, width), jnp.float32),
        in_specs=[pl.BlockSpec(memory_space=pltpu.VMEM)] * 3
        + [pl.BlockSpec(memory_space=pltpu.SMEM)],
        out_specs=pl.BlockSpec(memory_space=pltpu.VMEM),
        scratch_shapes=[
            vmem((2, ffw, slots), jnp.bfloat16),
            vmem((2, chunks, slots, w), jnp.bfloat16),
            vmem((chunks, slots, w), jnp.bfloat16),
            vmem((2, units, half // PARTS, w), jnp.bfloat16),
            vmem((2, units, half // PARTS, w), jnp.bfloat16),
            vmem((2, units, half // PARTS, w), jnp.bfloat16),
            vmem((half // PARTS, w), jnp.float32),
            vmem((units, n_outer, part_groups * owned, w), jnp.bfloat16),
            vmem((units, n_outer, part_groups * owned, w), jnp.bfloat16),
            vmem((part_groups, 2 * owned, w), jnp.float32),
            vmem((units // 2, part_groups, 2 * owned, w), jnp.bfloat16),
            vmem((2, chunks // 2, 2 * owned, w), jnp.bfloat16),
            dma, dma,
            dma((chunks,)), dma((chunks,)),
            dma((2, units)), dma((2, units)),
            dma((units, n_outer)), dma((units, n_outer)),
            dma((units // 2, part_groups)), dma((2, chunks // 2)),
        ],
        compiler_params=pltpu.CompilerParams(
            collective_id=0, has_side_effects=True, vmem_limit_bytes=56 * 1024 * 1024
        ),
        cost_estimate=pl.CostEstimate(
            flops=2 * slots * ffw * width, bytes_accessed=8 << 20, transcendentals=0
        ),
    )(activations, upstream, combine.reshape(1, slots), counts)


def solution(mesh):
    n_outer, n_node = mesh.shape["outer"], mesh.shape["node"]

    def body(activations, upstream, combine, counts):
        ffw, width = activations.shape[1], upstream.shape[1]
        owned = ffw // (n_outer * n_node)
        fits = (
            n_node >= 4
            and owned % 8 == 0
            and (owned * n_outer) % 16 == 0
            and n_node % (2 * PARTS) == 0
            and (owned * n_node // (2 * PARTS)) % 16 == 0
            and (width // 2) % (2 * CHUNK) == 0
        )
        if fits:
            return fused_body(n_outer, n_node, activations, upstream, combine, counts)
        return plain_body(activations, upstream, combine, counts)

    return jax.shard_map(
        body,
        mesh=mesh,
        in_specs=(
            P(("outer", "node"), None),
            P(("outer", "node"), None),
            P(("outer", "node")),
            P(("outer", "node")),
        ),
        out_specs=P(("node", "outer"), None),
        check_vma=False,
    )
```

```python
import functools
import jax
import jax.numpy as jnp
from jax import lax
from jax.experimental import pallas as pl
from jax.experimental.pallas import tpu as pltpu
from jax.sharding import PartitionSpec as P

BLOCK = 128
CHUNK = 128
PARTS = 1
HOP_LAG = 2
SUM_LAG = 3
AHEAD = 2
MESH = pl.DeviceIdType.MESH


def plain_body(activations, upstream, combine, counts):
    slots = activations.shape[0]
    width = upstream.shape[1]
    live = lax.iota(jnp.int32, slots) < counts[0]
    factor = jnp.where(live, combine, jnp.zeros_like(combine))
    scaled = (upstream.astype(jnp.float32) * factor[:, None]).astype(jnp.bfloat16)
    shard_rows = activations.shape[1] // lax.axis_size("node")
    partial_value = lax.dot_general(
        activations, scaled, (((0,), (0,)), ((), ())), preferred_element_type=jnp.float32
    )
    replica = lax.psum_scatter(
        partial_value.astype(jnp.bfloat16), "node", scatter_dimension=0, tiled=True
    ).astype(jnp.float32)
    blocks = replica.reshape(shard_rows, width // BLOCK, BLOCK)
    amax = jnp.max(jnp.abs(blocks), axis=2) + 1e-06
    scale_low = lax.optimization_barrier(amax.astype(jnp.bfloat16))
    quant = (blocks / scale_low.astype(jnp.float32)[..., None]).astype(jnp.bfloat16)
    quant = quant.reshape(shard_rows, width)
    got_quant, got_scale = (
        lax.all_to_all(quant, "outer", split_axis=0, concat_axis=0, tiled=True),
        lax.all_to_all(scale_low, "outer", split_axis=0, concat_axis=0, tiled=True),
    )
    sources = lax.axis_size("outer")
    owned = shard_rows // sources
    values = got_quant.astype(jnp.float32).reshape(sources, owned, width // BLOCK, BLOCK)
    scales = got_scale.astype(jnp.float32).reshape(sources, owned, width // BLOCK)
    restored = values * scales[..., None]
    return jnp.sum(restored, axis=0).reshape(owned, width)


def kernel(
    n_outer, n_node, chunks, w,
    acts_ref, up_ref, combine_ref, counts_ref, out_ref,
    acts_t, mine, theirs, part, got, summed, back, to_peers, from_peers, stash, to_owners, from_ends,
    a_send, a_recv, s_send, s_recv, z_send, z_recv, c_send, c_recv, d_send, d_recv,
):
    slots = acts_ref.shape[0]
    line = n_node // 2
    half = acts_t.shape[1] // 2
    groups = n_node // 2
    units = PARTS * chunks
    part_groups = groups // PARTS
    owned = out_ref.shape[0]
    group_rows = owned * n_outer
    cols = chunks * w
    o = lax.axis_index("outer")
    n = lax.axis_index("node")
    c, k = n // 2, n % 2
    sibling = c * 2 + (1 - k)
    at_end = jnp.logical_or(c == 0, c == line - 1)
    side = jnp.where(c == 0, 0, 1)

    barrier = pltpu.get_barrier_semaphore()
    for step in range(1, n_node):
        pl.semaphore_signal(
            barrier, inc=1, device_id=(o, lax.rem(n + step, n_node)), device_id_type=MESH
        )
    for step in range(1, n_outer):
        pl.semaphore_signal(
            barrier, inc=1, device_id=(lax.rem(o + step, n_outer), n), device_id_type=MESH
        )

    acts_t[0] = acts_ref[...].T
    live = lax.broadcasted_iota(jnp.int32, (1, slots), 1) < counts_ref[0]
    factor = jnp.where(live, combine_ref[...], 0.0)
    factor = jnp.broadcast_to(factor, (BLOCK, slots)).T

    def scaled(column):
        parts = []
        for b in range(w // BLOCK):
            at = pl.ds(pl.multiple_of(column + b * BLOCK, BLOCK), BLOCK)
            parts.append((up_ref[:, at].astype(jnp.float32) * factor).astype(jnp.bfloat16))
        return jnp.concatenate(parts, axis=1) if len(parts) > 1 else parts[0]

    pl.semaphore_wait(barrier, n_node + n_outer - 2)

    def acts_copy():
        return pltpu.make_async_remote_copy(
            src_ref=acts_t.at[0], dst_ref=acts_t.at[1], send_sem=a_send, recv_sem=a_recv,
            device_id=(o, sibling), device_id_type=MESH,
        )

    def scaled_copy(j):
        return pltpu.make_async_remote_copy(
            src_ref=theirs.at[j], dst_ref=mine.at[1, j],
            send_sem=s_send.at[j], recv_sem=s_recv.at[j],
            device_id=(o, sibling), device_id_type=MESH,
        )

    def chain_copy(way, j, source):
        onward = c - 1 if way == 0 else c + 1
        return pltpu.make_async_remote_copy(
            src_ref=source.at[way, j], dst_ref=got.at[way, j],
            send_sem=z_send.at[way, j], recv_sem=z_recv.at[way, j],
            device_id=(o, onward * 2 + k), device_id_type=MESH,
        )

    def peer_copy(j, to, slot):
        return pltpu.make_async_remote_copy(
            src_ref=to_peers.at[j, to], dst_ref=from_peers.at[j, slot],
            send_sem=c_send.at[j, to], recv_sem=c_recv.at[j, slot],
            device_id=(to, n), device_id_type=MESH,
        )

    def owner_of(unit, g):
        p = unit // chunks
        return side * groups + jnp.where(side == 0, PARTS - 1 - p, p) * part_groups + g

    def owner_copy(pair, g, core, owner):
        q = lax.rem(pair, chunks // 2)
        return pltpu.make_async_remote_copy(
            src_ref=to_owners.at[pair, g], dst_ref=from_ends.at[core, q],
            send_sem=d_send.at[pair, g], recv_sem=d_recv.at[core, q],
            device_id=(o, owner), device_id_type=MESH,
        )

    acts_copy().start()

    @pl.loop(0, chunks)
    def _(j):
        theirs[j] = scaled((1 - k) * cols + j * w)
        scaled_copy(j).start()

    acts_copy().wait_recv()

    def chain_step(way, t):
        lag = (line - 1 - c if way == 0 else c) * HOP_LAG
        first = lag == 0
        last = lag == (line - 1) * HOP_LAG
        j = t - lag
        inside = jnp.logical_and(j >= 0, j < units)

        @pl.when(jnp.logical_and(inside, jnp.logical_not(jnp.logical_or(first, last))))
        def _():
            chain_copy(way, j, part).wait_recv()
            summed[way, j] = (
                got[way, j].astype(jnp.float32) + part[way, j].astype(jnp.float32)
            ).astype(jnp.bfloat16)
            chain_copy(way, j, summed).start()

    def quantise_step(t):
        j = t - (line - 1) * HOP_LAG

        @pl.when(jnp.logical_and(at_end, jnp.logical_and(j >= 0, j < units)))
        def _():
            for way in range(2):

                @pl.when(side == way)
                def _(way=way):
                    chain_copy(way, j, part).wait_recv()

            for g in range(part_groups):
                rows = pl.ds(g * group_rows, group_rows)
                replica = got[side, j, rows, :].astype(jnp.float32) + part[
                    side, j, rows, :
                ].astype(jnp.float32)
                for b in range(w // BLOCK):
                    block = replica[:, b * BLOCK : (b + 1) * BLOCK]
                    amax = jnp.max(jnp.abs(block), axis=1, keepdims=True) + 1e-06
                    scale = amax.astype(jnp.bfloat16).astype(jnp.float32)
                    quant = (block / scale).astype(jnp.bfloat16)
                    back[rows, b * BLOCK : (b + 1) * BLOCK] = quant.astype(jnp.float32) * scale
            for to in range(n_outer):
                rows = [
                    back[g * group_rows + to * owned : g * group_rows + (to + 1) * owned, :]
                    for g in range(part_groups)
                ]
                rows = jnp.concatenate(rows, axis=0).astype(jnp.bfloat16)

                @pl.when(o == to)
                def _(rows=rows, to=to):
                    from_peers[j, to] = rows

                @pl.when(o != to)
                def _(rows=rows, to=to):
                    to_peers[j, to] = rows
                    peer_copy(j, to, o).start()

    def sum_step(t):
        j = t - (line - 1) * HOP_LAG - SUM_LAG

        @pl.when(jnp.logical_and(at_end, jnp.logical_and(j >= 0, j < units)))
        def _():
            for slot in range(n_outer):

                @pl.when(o != slot)
                def _(slot=slot):
                    peer_copy(j, lax.rem(o + 1, n_outer), slot).wait_recv()

            total = from_peers[j, 0].astype(jnp.float32)
            for slot in range(1, n_outer):
                total = total + from_peers[j, slot].astype(jnp.float32)
            for g in range(part_groups):
                owner = owner_of(j, g)
                rows = total[g * owned : (g + 1) * owned, :]

                @pl.when(owner == n)
                def _(rows=rows):
                    at = pl.ds(pl.multiple_of(k * cols + lax.rem(j, chunks) * w, BLOCK), w)
                    out_ref[:, at] = rows

                @pl.when(owner != n)
                def _(rows=rows, g=g):
                    stash[g, pl.ds(pl.multiple_of(lax.rem(j, 2) * owned, 8), owned), :] = rows

                @pl.when(jnp.logical_and(owner != n, lax.rem(j, 2) == 1))
                def _(g=g, owner=owner):
                    to_owners[j // 2, g] = stash[g].astype(jnp.bfloat16)
                    owner_copy(j // 2, g, k, owner).start()

    @pl.loop(0, units + (line - 1) * HOP_LAG + SUM_LAG)
    def _(t):
        @pl.when(t * AHEAD < chunks)
        def _():
            @pl.loop(t * AHEAD, t * AHEAD + AHEAD)
            def _(t):
                mine[0, t] = scaled(k * cols + t * w)
                scaled_copy(t).wait_recv()
                value = jnp.dot(
                    acts_t[0], mine[0, t], preferred_element_type=jnp.float32
                ) + jnp.dot(acts_t[1], mine[1, t], preferred_element_type=jnp.float32)
                value = value.astype(jnp.bfloat16)
                size = half // PARTS
                for p in range(PARTS):
                    low = (PARTS - 1 - p) * size
                    part[0, p * chunks + t] = value[low : low + size]
                    part[1, p * chunks + t] = value[half + p * size : half + (p + 1) * size]

                @pl.when(c == line - 1)
                def _():
                    chain_copy(0, t, part).start()

                @pl.when(c == 0)
                def _():
                    chain_copy(1, t, part).start()

        chain_step(0, t)
        chain_step(1, t)
        sum_step(t)
        quantise_step(t)

    end_chip = jnp.where(n < groups, 0, line - 1)

    acts_copy().wait_send()

    @pl.loop(0, units)
    def _(j):
        @pl.when(c > 0)
        def _():
            chain_copy(0, j, part).wait_send()

        @pl.when(c < line - 1)
        def _():
            chain_copy(1, j, part).wait_send()

        @pl.when(at_end)
        def _():
            for to in range(n_outer):

                @pl.when(o != to)
                def _(to=to):
                    peer_copy(j, to, o).wait_send()

            for g in range(part_groups):

                @pl.when(jnp.logical_and(owner_of(j, g) != n, lax.rem(j, 2) == 1))
                def _(g=g):
                    owner_copy(j // 2, g, k, sibling).wait_send()

    @pl.loop(0, chunks)
    def _(j):
        scaled_copy(j).wait_send()

    @pl.loop(0, chunks // 2)
    def _(q):
        for core in range(2):

            @pl.when(end_chip * 2 + core != n)
            def _(core=core):
                owner_copy(q, 0, core, sibling).wait_recv()
                both = from_ends[core, q].astype(jnp.float32)
                for b in range(2):
                    at = pl.ds(pl.multiple_of(core * cols + (2 * q + b) * w, BLOCK), w)
                    out_ref[:, at] = both[b * owned : (b + 1) * owned]


def fused_body(n_outer, n_node, activations, upstream, combine, counts):
    slots, ffw = activations.shape
    width = upstream.shape[1]
    owned = ffw // (n_outer * n_node)
    half, cols = ffw // 2, width // 2
    w = CHUNK
    chunks = cols // w
    units = PARTS * chunks
    part_groups = n_node // 2 // PARTS
    dma = pltpu.SemaphoreType.DMA
    vmem = pltpu.VMEM
    return pl.pallas_call(
        functools.partial(kernel, n_outer, n_node, chunks, w),
        out_shape=jax.ShapeDtypeStruct((owned, width), jnp.float32),
        in_specs=[pl.BlockSpec(memory_space=pltpu.VMEM)] * 3
        + [pl.BlockSpec(memory_space=pltpu.SMEM)],
        out_specs=pl.BlockSpec(memory_space=pltpu.VMEM),
        scratch_shapes=[
            vmem((2, ffw, slots), jnp.bfloat16),
            vmem((2, chunks, slots, w), jnp.bfloat16),
            vmem((chunks, slots, w), jnp.bfloat16),
            vmem((2, units, half // PARTS, w), jnp.bfloat16),
            vmem((2, units, half // PARTS, w), jnp.bfloat16),
            vmem((2, units, half // PARTS, w), jnp.bfloat16),
            vmem((half // PARTS, w), jnp.float32),
            vmem((units, n_outer, part_groups * owned, w), jnp.bfloat16),
            vmem((units, n_outer, part_groups * owned, w), jnp.bfloat16),
            vmem((part_groups, 2 * owned, w), jnp.float32),
            vmem((units // 2, part_groups, 2 * owned, w), jnp.bfloat16),
            vmem((2, chunks // 2, 2 * owned, w), jnp.bfloat16),
            dma, dma,
            dma((chunks,)), dma((chunks,)),
            dma((2, units)), dma((2, units)),
            dma((units, n_outer)), dma((units, n_outer)),
            dma((units // 2, part_groups)), dma((2, chunks // 2)),
        ],
        compiler_params=pltpu.CompilerParams(
            collective_id=0, has_side_effects=True, vmem_limit_bytes=56 * 1024 * 1024
        ),
        cost_estimate=pl.CostEstimate(
            flops=2 * slots * ffw * width, bytes_accessed=8 << 20, transcendentals=0
        ),
    )(activations, upstream, combine.reshape(1, slots), counts)


def solution(mesh):
    n_outer, n_node = mesh.shape["outer"], mesh.shape["node"]

    def body(activations, upstream, combine, counts):
        ffw, width = activations.shape[1], upstream.shape[1]
        owned = ffw // (n_outer * n_node)
        fits = (
            n_node >= 4
            and owned % 8 == 0
            and (owned * n_outer) % 16 == 0
            and n_node % (2 * PARTS) == 0
            and (owned * n_node // (2 * PARTS)) % 16 == 0
            and (width // 2) % (2 * CHUNK) == 0
            and (width // 2 // CHUNK) % AHEAD == 0
        )
        if fits:
            return fused_body(n_outer, n_node, activations, upstream, combine, counts)
        return plain_body(activations, upstream, combine, counts)

    return jax.shard_map(
        body,
        mesh=mesh,
        in_specs=(
            P(("outer", "node"), None),
            P(("outer", "node"), None),
            P(("outer", "node")),
            P(("outer", "node")),
        ),
        out_specs=P(("node", "outer"), None),
        check_vma=False,
    )
```
